512 devices in a mesh: seq: 64 (over z, y), dp: 8 (over x, core).
Axes of the slice: x: 4, y: 4, z: 16, core: 2. Of those that a mesh axis runs over, the one named last changes fastest.
Arguments:
- phonemes: bfloat16 [32768, 1024], P(('dp', 'seq')), parts along dimension 0, may hold values from -6 to 6
- spread: float32 [32768], P(('dp', 'seq')), parts along dimension 0, may hold values from 2 to 8
- durations: int32 [512, 64], P(('dp', 'seq')), parts along dimension 0, may hold values from 1 to 32, 512 in all within a row
- norm_gain: float32 [1024], replicated, may hold values from 0.1 to 1.9
- w_query: bfloat16 [1024, 1024], P('seq')
- w_key: bfloat16 [1024, 1024], P('seq'), may hold values from -0.1875 to 0.1875
- w_value: bfloat16 [1024, 1024], P('seq'), may hold values from -0.1875 to 0.1875
- w_out: bfloat16 [1024, 1024], P('seq'), may hold values from -0.1875 to 0.1875
Outputs:
- frames_out: bfloat16 [262144, 1024], P(('dp', 'seq')), parts along dimension 0
The draws below stay inside these ranges and needn't reach their ends.
There are 8 independent parts, one for each index of `dp`. The reference program is written for one: setup_inputs(seed, part) draws one part's arguments, and reference() takes and returns one part's arrays. A program takes and returns all parts, laid end to end along the dimension named above; an argument that names none is the same for every part. Nothing has to cross between parts.
Inputs may be any that keep to these rules, and one draw needn't show every extreme that they name: Each row holds the durations of the 64 phonemes of one block of 512 frames: it sums to 512 and its largest entry is 32.
All inputs are finite; a program needn't handle non-finite values.
Results may differ from the reference program's by a relative error of at most 0.035.
Values may be sent and summed in bfloat16 or wider, within the bound.
A program may use at most 128 MiB of HBM per device.

```python
import math
import jax
import jax.numpy as jnp
import numpy as np
from jax import lax

D = 1024
HEADS = 16
HEAD_DIM = 64
FR_DEV = 512
MAXD = 32
RADIUS = 32
WIN = 128
PH_DEV = 64
PHONES = 4096
FRAMES = 32768
N_SEQ = 64


def draw_w_query(key, part):
    key = jax.random.fold_in(key, 11)
    base = jax.random.normal(key, (D, D), jnp.float32) * (1.0 / D ** 0.5)
    return base.astype(jnp.bfloat16)


def steps_of(key, dims, pieces, smallest, largest):
    def one(position, parts):
        steps = jax.random.uniform(jax.random.fold_in(jax.random.fold_in(key, 6), position), (parts,), jnp.float32, smallest / len(pieces), largest / len(pieces))
        return jnp.repeat(jnp.exp(steps), dims[position] // parts).reshape((-1,) + (1,) * (len(dims) - position - 1))

    gain = one(*pieces[0])
    for cut in pieces[1:]:
        gain = gain * one(*cut)
    return gain


def profile(amount, total, bound, lean):
    loads = [(1 << 20) // math.isqrt(rank ** lean) + 1 for rank in range(2, amount + 1)]
    surplus, holding = total - bound - (amount - 1), [1] * (amount - 1)
    while surplus > 0:
        free = [i for i in range(amount - 1) if holding[i] < bound]
        whole, left = sum([loads[i] for i in free]), surplus
        for i in free:
            extra = min(bound - holding[i], max(1, left * loads[i] // whole), surplus)
            holding[i] = holding[i] + extra
            surplus = surplus - extra
    return np.array([bound] + holding)


def ragged_sizes(stream_key, amount, total, bound, slope):
    if amount == 2:
        one = jax.random.randint(stream_key, (), max(1, total - bound), min(bound, total - 1) + 1)
        return jnp.stack([one, total - one])
    tallies = jnp.asarray(profile(amount, total, bound, slope), jnp.int32)
    couples = (amount - 1) // 2
    giver, sink = tallies[1:1 + 2 * couples:2], tallies[2:2 + 2 * couples:2]
    room = jnp.minimum(giver - 1, bound - sink)
    passed = jax.random.randint(jax.random.fold_in(stream_key, 1), (couples,), 0, 1 << 20) % (room + 1)
    tallies = tallies.at[1:1 + 2 * couples:2].set(giver - passed).at[2:2 + 2 * couples:2].set(sink + passed)
    return tallies[jax.random.permutation(jax.random.fold_in(stream_key, 2), amount)]


def gaussian(stream_key, dims, deviation, bound, cuts=(), kind=jnp.bfloat16):
    entries = deviation * jax.random.normal(stream_key, dims, jnp.float32)
    if cuts:
        entries = entries * steps_of(stream_key, dims, cuts, -0.22, 0.18)
    return jnp.clip(entries, -bound, bound).astype(kind)


def setup_inputs(seed: int = 0, part: int = 0) -> dict:
    streams_of = jax.random.split(jax.random.key(seed), 9)
    own_keys = jax.random.split(jax.random.fold_in(streams_of[8], part), 9)
    phonemes = gaussian(own_keys[0], (PHONES, D), 1.0, 6.0, ((0, 64),))
    spread = jnp.clip(jnp.exp(math.log(8.0) - 1.3862944 * jax.random.uniform(own_keys[1], (PHONES,), jnp.float32) ** steps_of(own_keys[1], (PHONES,), ((0, 64),), -0.2, 0.2)), 2.0, 8.0)
    durations = jax.vmap(lambda own: ragged_sizes(own, PH_DEV, FR_DEV, MAXD, 2))(jax.random.split(own_keys[2], N_SEQ)).reshape((N_SEQ, PH_DEV)).astype(jnp.int32)
    norm_gain = jnp.clip(1.0 + 0.18 * jax.random.normal(streams_of[3], (D,), jnp.float32), 0.1, 1.9)
    w_query = draw_w_query(jax.random.fold_in(streams_of[8], 71), part)
    w_key = gaussian(streams_of[5], (D, D), D ** -0.5, 0.1875, ((0, 64),))
    w_value = gaussian(streams_of[6], (D, D), D ** -0.5, 0.1875, ((0, 64),))
    w_out = gaussian(streams_of[7], (D, D), D ** -0.5, 0.1875, ((0, 64),))
    return {"phonemes": phonemes, "spread": spread, "durations": durations, "norm_gain": norm_gain, "w_query": w_query, "w_key": w_key, "w_value": w_value, "w_out": w_out}


def band_weights(frame_pos, centers, spread, usable):
    offset = frame_pos[:, None] - centers[None, :]
    sigma = jnp.where(usable, spread, 1.0)
    inside = usable[None, :] & (jnp.abs(offset) <= RADIUS)
    return jnp.where(inside, jnp.exp(-(offset * offset) / (2.0 * sigma * sigma)[None, :]), 0.0)

def attend(query, keys, values, allowed):
    row_count = query.shape[0]
    key_count = keys.shape[0]
    q_heads = query.astype(jnp.float32).reshape(row_count, HEADS, HEAD_DIM)
    k_heads = keys.astype(jnp.float32).reshape(key_count, HEADS, HEAD_DIM)
    v_heads = values.astype(jnp.float32).reshape(key_count, HEADS, HEAD_DIM)
    scores = jnp.einsum('thd,uhd->htu', q_heads, k_heads) * (1.0 / math.sqrt(HEAD_DIM))
    scores = jnp.where(allowed[None], scores, -1e+30)
    row_max = lax.optimization_barrier(jnp.max(scores, axis=2, keepdims=True))
    raised = jnp.exp(scores - row_max)
    weights_bf = (raised / lax.optimization_barrier(jnp.sum(raised, axis=2, keepdims=True))).astype(jnp.bfloat16)
    mixture = jnp.einsum('htu,uhd->thd', weights_bf.astype(jnp.float32), v_heads)
    return mixture.reshape(row_count, HEADS * HEAD_DIM).astype(jnp.bfloat16)

def reference(phonemes, spread, durations, norm_gain, w_query, w_key, w_value, w_out):
    flat_dur = durations.reshape(-1)
    end_frames = jnp.cumsum(flat_dur).astype(jnp.int32)
    centers = end_frames.astype(jnp.float32) - flat_dur.astype(jnp.float32) * 0.5
    rows_pad = jnp.pad(phonemes, ((RADIUS, RADIUS), (0, 0)))
    centers_pad = jnp.pad(centers, (RADIUS, RADIUS))
    spread_pad = jnp.pad(spread, (RADIUS, RADIUS))
    usable_pad = jnp.pad(jnp.ones((PHONES,), dtype=bool), (RADIUS, RADIUS))
    span_rows = PH_DEV + 2 * RADIUS

    def upsample_block(block):
        first = block * PH_DEV
        rows_here = lax.dynamic_slice_in_dim(rows_pad, first, span_rows, 0)
        cent_here = lax.dynamic_slice_in_dim(centers_pad, first, span_rows, 0)
        spread_here = lax.dynamic_slice_in_dim(spread_pad, first, span_rows, 0)
        usable_here = lax.dynamic_slice_in_dim(usable_pad, first, span_rows, 0)
        frame_pos = (block * FR_DEV + jnp.arange(FR_DEV, dtype=jnp.int32)).astype(jnp.float32) + 0.5
        band = band_weights(frame_pos, cent_here, spread_here, usable_here)
        totals = lax.optimization_barrier(jnp.sum(band, axis=1))
        mixture = jnp.dot(band.astype(jnp.bfloat16), rows_here, preferred_element_type=jnp.float32) / totals[:, None]
        return mixture.astype(jnp.bfloat16)
    blocks = jnp.arange(N_SEQ, dtype=jnp.int32)
    upsampled = lax.map(upsample_block, blocks).reshape(FRAMES, D)
    wide_f32 = upsampled.astype(jnp.float32)
    normed = (wide_f32 * lax.rsqrt(lax.optimization_barrier(jnp.mean(wide_f32 * wide_f32, axis=1, keepdims=True)) + 1e-06) * norm_gain).astype(jnp.bfloat16)
    query = jnp.dot(normed, w_query, preferred_element_type=jnp.float32).astype(jnp.bfloat16)
    key_rows = jnp.dot(normed, w_key, preferred_element_type=jnp.float32).astype(jnp.bfloat16)
    value_rows = jnp.dot(normed, w_value, preferred_element_type=jnp.float32).astype(jnp.bfloat16)
    keys_pad = jnp.pad(key_rows, ((WIN, WIN), (0, 0)))
    values_pad = jnp.pad(value_rows, ((WIN, WIN), (0, 0)))

    def attend_block(block):
        first = block * FR_DEV
        q_block = lax.dynamic_slice_in_dim(query, first, FR_DEV, 0)
        k_block = lax.dynamic_slice_in_dim(keys_pad, first, FR_DEV + 2 * WIN, 0)
        v_block = lax.dynamic_slice_in_dim(values_pad, first, FR_DEV + 2 * WIN, 0)
        q_pos = first + jnp.arange(FR_DEV, dtype=jnp.int32)
        k_pos = first - WIN + jnp.arange(FR_DEV + 2 * WIN, dtype=jnp.int32)
        allowed = (k_pos >= 0)[None, :] & (k_pos < FRAMES)[None, :] & (jnp.abs(q_pos[:, None] - k_pos[None, :]) <= WIN)
        attended = attend(q_block, k_block, v_block, allowed)
        resid = lax.dynamic_slice_in_dim(wide_f32, first, FR_DEV, 0)
        return (resid + jnp.dot(attended, w_out, preferred_element_type=jnp.float32)).astype(jnp.bfloat16)
    return lax.map(attend_block, blocks).reshape(FRAMES, D)
```

```python
import functools
import math

import jax
import jax.numpy as jnp
from jax import lax
from jax.experimental import pallas as pl
from jax.experimental.pallas import tpu as pltpu
from jax.sharding import PartitionSpec as P

MESH = pl.DeviceIdType.MESH
NZ, NY, NX = 16, 4, 4
D = 1024
FR = 512
PH = 64
RADIUS = 32.0
WIN = 128
KEYS = FR + 2 * WIN
BLK = 128
SPAN = BLK + 2 * WIN
GROUP = 256
SCALE = math.log2(math.e) / 8.0
VAL, QRY, KEY, OUT = 0, 1, 2, 3


def kernel(ph, spread, dur, gain, w_val, w_qry, w_key, w_out, out,
           full, phx, aux, auxs, up, qs, ks, vs, att,
           zs, zr, ms, mr, ls, lr, cs, cr, own, hs, hr, asem, arem):
    s = lax.axis_index("seq")
    d = lax.axis_index("dp")
    z, y, x, c = s // NY, s % NY, d // 2, d % 2
    shards = (w_val, w_qry, w_key, w_out)

    def at(dz, dy, dx, dc):
        zz, yy, xx, cc = (z + dz) % NZ, (y + dy) % NY, (x + dx) % NX, (c + dc) % 2
        return (zz * NY + yy, xx * 2 + cc)

    after = ((s + 1) % (NZ * NY), d)
    before = ((s + NZ * NY - 1) % (NZ * NY), d)

    barrier = pltpu.get_barrier_semaphore()

    def greet(dev):
        pl.semaphore_signal(barrier, inc=1, device_id=dev, device_id_type=MESH)

    for k in range(1, NZ):
        greet(at(k, 0, 0, 0))
    for k in range(1, NY):
        greet(at(0, k, 0, 0))
        greet(at(0, 0, k, 0))
    greet(at(0, 0, 0, 1))
    greet(after)
    greet(before)

    durf = dur[...].astype(jnp.float32)
    row = lax.broadcasted_iota(jnp.int32, (PH, PH), 0)
    col = lax.broadcasted_iota(jnp.int32, (PH, PH), 1)
    tri = jnp.where(row <= col, 1.0, 0.0).astype(jnp.bfloat16)
    ends = jnp.dot(jnp.broadcast_to(durf, (8, PH)).astype(jnp.bfloat16), tri,
                   preferred_element_type=jnp.float32)
    auxs[...] = jnp.zeros_like(auxs)
    auxs[0:1, 0:PH] = ends[0:1] - durf * 0.5
    auxs[1:2, 0:PH] = spread[...]

    pl.semaphore_wait(barrier, (NZ - 1) + (NY - 1) + (NX - 1) + 1 + 2)

    def remote(src, dst, ssem, rsem, dev):
        return pltpu.make_async_remote_copy(
            src_ref=src, dst_ref=dst, send_sem=ssem, recv_sem=rsem, device_id=dev, device_id_type=MESH)

    def waited(ref, sem):
        pltpu.make_async_copy(ref, ref, sem).wait()

    remote(auxs, aux.at[0], asem.at[0], arem.at[0], after).start()
    remote(auxs, aux.at[2], asem.at[1], arem.at[1], before).start()
    remote(ph, phx.at[0], hs.at[0], hr.at[0], after).start()
    remote(ph, phx.at[2], hs.at[1], hr.at[1], before).start()

    columns = pl.ds(pl.multiple_of(d * 128, 128), 128)
    for w in range(4):
        piece = shards[w].at[:, columns]
        pltpu.make_async_copy(piece, full.at[w, x, c, z, y], own.at[w]).start()

        def send_z(j, carry, w=w, piece=piece):
            half = (j + 1) // 2
            k = 8 + half * (1 - 2 * (j % 2))
            remote(piece, full.at[w, x, c, z, y], zs.at[w], zr.at[w], at(k, 0, 0, 0)).start()
            return carry

        lax.fori_loop(0, NZ - 1, send_z, 0)
    pltpu.make_async_copy(ph, phx.at[1], own.at[4]).start()
    aux[1] = auxs[...]

    def mid(w):
        pltpu.make_async_copy(shards[w].at[:, columns], full.at[w, x, c, z, y], own.at[w]).wait()
        waited(full.at[w, x, c, pl.ds(0, NZ - 1), 0], zr.at[w])
        for k in (2, 1, 3):
            remote(full.at[w, x, c, :, y], full.at[w, x, c, :, y], ms.at[w], mr.at[w],
                   at(0, k * (1 - c), k * c, 0)).start()

    def portion(w, cc, k):
        if cc == 0:
            return full.at[w, (x + NX - k) % NX, 0]
        return full.at[w, :, 1, :, (y + NY - k) % NY]

    def each_core(body):
        for cc in range(2):
            pl.when(c == cc)(functools.partial(body, cc))

    def last(w):
        waited(full.at[w, x, c, pl.ds(0, 12)], mr.at[w])

        def body(cc):
            mine = portion(w, cc, 0)
            for k in (1, 3, 2):
                remote(mine, mine, ls.at[w], lr.at[w * 3 + k - 1],
                       at(0, k * cc, k * (1 - cc), 0)).start()
            remote(mine, mine, cs.at[w], cr.at[w], at(0, 0, 0, 1)).start()

        each_core(body)

    def swap(w):
        def body(cc):
            for k in (1, 3, 2):
                got = portion(w, cc, k)
                waited(got, lr.at[w * 3 + k - 1])
                remote(got, got, cs.at[w], cr.at[w], at(0, 0, 0, 1)).start()

        each_core(body)

    def whole(w):
        waited(full.at[w, :, 0], cr.at[w])

    def weight(w, g):
        return jnp.concatenate(
            [full[w, g, 0].reshape(D, 128), full[w, g, 1].reshape(D, 128)], axis=1)

    waited(aux.at[0], arem.at[0])
    waited(aux.at[2], arem.at[1])
    cent = jnp.concatenate(
        [aux[0, 0:1, 0:PH] - FR, aux[1, 0:1, 0:PH], aux[2, 0:1, 0:PH] + FR], axis=1)
    sig = jnp.concatenate(
        [aux[0, 1:2, 0:PH], aux[1, 1:2, 0:PH], aux[2, 1:2, 0:PH]], axis=1)
    slot = lax.broadcasted_iota(jnp.int32, (1, 3 * PH), 1)
    usable = ((slot >= PH) | (s > 0)) & ((slot < 2 * PH) | (s < NZ * NY - 1))
    reach = jnp.where(usable, RADIUS, -1.0)
    fall = -0.5 / (sig * sig)
    frame = lax.broadcasted_iota(jnp.int32, (KEYS, 3 * PH), 0).astype(jnp.float32) + (0.5 - WIN)
    gap = frame - cent
    band = jnp.where(jnp.abs(gap) <= reach, jnp.exp(gap * gap * fall), 0.0)
    total = jnp.sum(band, axis=1, keepdims=True)
    inv = jnp.where(total > 1e-16, 1.0 / total, 0.0)
    band_bf = band.astype(jnp.bfloat16)
    mid(0)
    waited(phx.at[0], hr.at[0])
    waited(phx.at[2], hr.at[1])
    pltpu.make_async_copy(ph, phx.at[1], own.at[4]).wait()
    rows = phx[...].reshape(3 * PH, D)
    lifted = (jnp.dot(band_bf, rows, preferred_element_type=jnp.float32) * inv).astype(jnp.bfloat16)
    up[...] = lifted[WIN:WIN + FR]
    wide = lifted.astype(jnp.float32)
    norm = lax.rsqrt(jnp.mean(wide * wide, axis=1, keepdims=True) + 1e-6) * inv
    gained = (rows.astype(jnp.float32) * gain[...]).astype(jnp.bfloat16)

    mid(1)
    last(0)
    mid(2)
    last(1)
    mid(3)
    last(2)
    last(3)

    def project(w, band_rows, scale, dest):
        for g in range(4):
            part = jnp.dot(gained, weight(w, g), preferred_element_type=jnp.float32).astype(jnp.bfloat16)
            dest[:, g * GROUP:(g + 1) * GROUP] = (
                jnp.dot(band_rows, part, preferred_element_type=jnp.float32) * scale).astype(jnp.bfloat16)

    swap(0)
    whole(0)
    project(VAL, band_bf, norm, vs)
    swap(1)
    whole(1)
    project(QRY, band_bf[WIN:WIN + FR], norm[WIN:WIN + FR] * SCALE, qs)
    swap(2)
    whole(2)
    project(KEY, band_bf, norm, ks)

    t_id = lax.broadcasted_iota(jnp.int32, (BLK, BLK), 0)
    u_id = lax.broadcasted_iota(jnp.int32, (BLK, BLK), 1)
    lane = lax.broadcasted_iota(jnp.int32, (BLK, GROUP), 1) // 64
    low = -1e30
    for g in range(4):
        if g == 2:
            swap(3)
        lanes = slice(g * GROUP, (g + 1) * GROUP)
        for b in range(4):
            q4 = qs[b * BLK:(b + 1) * BLK, lanes]
            k4 = ks[b * BLK:b * BLK + SPAN, lanes]
            v4 = vs[b * BLK:b * BLK + SPAN, lanes]
            head = u_id >= t_id
            tail = u_id <= t_id
            if b == 0:
                head = head & (s > 0)
            if b == 3:
                tail = tail & (s < NZ * NY - 1)
            head = jnp.where(head, 0.0, low)
            tail = jnp.where(tail, 0.0, low)
            stacked = jnp.concatenate([jnp.where(lane == h, q4, jnp.zeros_like(q4)) for h in range(4)], axis=0)
            scores = lax.dot_general(stacked, k4, (((1,), (1,)), ((), ())), preferred_element_type=jnp.float32)
            bias = jnp.concatenate([head, jnp.zeros((BLK, BLK), jnp.float32), tail], axis=1)
            scores = scores + jnp.concatenate([bias] * 4, axis=0)
            raised = jnp.exp2(scores - jnp.max(scores, axis=1, keepdims=True))
            scale = 1.0 / jnp.sum(raised, axis=1, keepdims=True)
            mixed = jnp.dot(raised.astype(jnp.bfloat16), v4, preferred_element_type=jnp.float32) * scale
            got = jnp.zeros((BLK, GROUP), jnp.float32)
            for h in range(4):
                got = jnp.where(lane == h, mixed[h * BLK:(h + 1) * BLK], got)
            att[b * BLK:(b + 1) * BLK, lanes] = got.astype(jnp.bfloat16)

    whole(3)
    for g in range(4):
        lanes = slice(g * GROUP, (g + 1) * GROUP)
        out[:, lanes] = (
            jnp.dot(att[...], weight(OUT, g), preferred_element_type=jnp.float32)
            + up[:, lanes].astype(jnp.float32)).astype(jnp.bfloat16)

    for i in range(2):
        waited(auxs, asem.at[i])
        waited(ph, hs.at[i])
    for w in range(4):
        waited(full.at[w, x, c, pl.ds(0, NZ - 1), 0], zs.at[w])
        waited(full.at[w, x, c, pl.ds(0, 12)], ms.at[w])
        waited(full.at[w, pl.ds(0, 3), c], ls.at[w])
        waited(full.at[w, :, c], cs.at[w])


def on_device(phonemes, spread, durations, norm_gain, w_query, w_key, w_value, w_out):
    vmem = pl.BlockSpec(memory_space=pltpu.VMEM)
    hbm = pl.BlockSpec(memory_space=pl.ANY)
    bf = jnp.bfloat16
    dma = pltpu.SemaphoreType.DMA
    return pl.pallas_call(
        kernel,
        out_shape=jax.ShapeDtypeStruct((FR, D), bf),
        in_specs=[hbm, vmem, vmem, vmem, hbm, hbm, hbm, hbm],
        out_specs=vmem,
        scratch_shapes=[
            pltpu.VMEM((4, NX, 2, NZ, NY, 16, 128), bf),
            pltpu.VMEM((3, PH, D), bf),
            pltpu.VMEM((3, 8, 128), jnp.float32),
            pltpu.VMEM((8, 128), jnp.float32),
            pltpu.VMEM((FR, D), bf),
            pltpu.VMEM((FR, D), bf),
            pltpu.VMEM((KEYS, D), bf),
            pltpu.VMEM((KEYS, D), bf),
            pltpu.VMEM((FR, D), bf),
            dma((4,)), dma((4,)), dma((4,)), dma((4,)), dma((4,)), dma((12,)),
            dma((4,)), dma((4,)), dma((5,)), dma((2,)), dma((2,)), dma((2,)), dma((2,)),
        ],
        compiler_params=pltpu.CompilerParams(
            collective_id=0, has_side_effects=True, vmem_limit_bytes=56 * 1024 * 1024),
        name="chapter_block",
    )(phonemes, spread.reshape(1, PH), durations, norm_gain.reshape(1, D),
      w_value, w_query, w_key, w_out)


def solution(mesh):
    placed = (
        P(("dp", "seq"), None),
        P(("dp", "seq")),
        P(("dp", "seq"), None),
        P(),
        P("seq", None),
        P("seq", None),
        P("seq", None),
        P("seq", None),
    )
    return jax.shard_map(
        on_device, mesh=mesh, in_specs=placed, out_specs=P(("dp", "seq"), None), check_vma=False
    )
```

```python
import functools
import math

import jax
import jax.numpy as jnp
from jax import lax
from jax.experimental import pallas as pl
from jax.experimental.pallas import tpu as pltpu
from jax.sharding import PartitionSpec as P

MESH = pl.DeviceIdType.MESH
NZ, NY, NX = 16, 4, 4
D = 1024
FR = 512
PH = 64
RADIUS = 32.0
WIN = 128
KEYS = FR + 2 * WIN
BLK = 128
SPAN = BLK + 2 * WIN
GROUP = 256
SCALE = math.log2(math.e) / 8.0
QRY, KEY, VAL, OUT = 0, 1, 2, 3


def kernel(ph, spread, dur, gain, w_qry, w_key, w_val, w_out, out,
           wb, wo, phx, phall, gall, sent, pall, aux, auxs, up, qs, ks, vs, probs, att,
           zs, zr, ms, mr, ls, lr, cs, cr, own, xs, xr, ps, pr, es, er, hs, hr, asem, arem):
    s = lax.axis_index("seq")
    d = lax.axis_index("dp")
    z, y, x, c = s // NY, s % NY, d // 2, d % 2
    shards = (w_qry, w_key, w_val, w_out)
    blocks = NZ * NY

    def at(dz, dy, dx, dc):
        zz, yy, xx, cc = (z + dz) % NZ, (y + dy) % NY, (x + dx) % NX, (c + dc) % 2
        return (zz * NY + yy, xx * 2 + cc)

    def beside(step, j):
        return ((s + blocks + step) % blocks, (d + j) % 8)

    barrier = pltpu.get_barrier_semaphore()

    def greet(dev):
        pl.semaphore_signal(barrier, inc=1, device_id=dev, device_id_type=MESH)

    for k in range(1, NZ):
        greet(at(k, 0, 0, 0))
    for k in range(1, NY):
        greet(at(0, k, 0, 0))
    for j in range(8):
        if j:
            greet(beside(0, j))
        greet(beside(1, j))
        greet(beside(-1, j))

    durf = dur[...].astype(jnp.float32)
    row = lax.broadcasted_iota(jnp.int32, (PH, PH), 0)
    col = lax.broadcasted_iota(jnp.int32, (PH, PH), 1)
    tri = jnp.where(row <= col, 1.0, 0.0).astype(jnp.bfloat16)
    ends = jnp.dot(jnp.broadcast_to(durf, (8, PH)).astype(jnp.bfloat16), tri,
                   preferred_element_type=jnp.float32)
    auxs[...] = jnp.zeros_like(auxs)
    auxs[0:1, 0:PH] = ends[0:1] - durf * 0.5
    auxs[1:2, 0:PH] = spread[...]
    aux[1] = auxs[...]

    pl.semaphore_wait(barrier, (NZ - 1) + (NY - 1) + 7 + 16)

    def remote(src, dst, ssem, rsem, dev):
        return pltpu.make_async_remote_copy(
            src_ref=src, dst_ref=dst, send_sem=ssem, recv_sem=rsem, device_id=dev, device_id_type=MESH)

    def waited(ref, sem):
        pltpu.make_async_copy(ref, ref, sem).wait()

    columns = pl.ds(pl.multiple_of(d * 128, 128), 128)

    def place(w):
        return wo.at[x, c, z, y] if w == OUT else wb.at[w, z, y]

    def start_z(w):
        piece = shards[w].at[:, columns]
        pltpu.make_async_copy(piece, place(w), own.at[w]).start()

        def send_z(j, carry):
            half = (j + 1) // 2
            k = 8 + half * (1 - 2 * (j % 2))
            remote(piece, place(w), zs.at[w], zr.at[w], at(k, 0, 0, 0)).start()
            return carry

        lax.fori_loop(0, NZ - 1, send_z, 0)

    start_z(QRY)
    remote(auxs, aux.at[0], asem.at[0], arem.at[0], beside(1, 0)).start()
    remote(auxs, aux.at[2], asem.at[1], arem.at[1], beside(-1, 0)).start()
    remote(ph, phx.at[0], hs.at[0], hr.at[0], beside(1, 0)).start()
    remote(ph, phx.at[2], hs.at[1], hr.at[1], beside(-1, 0)).start()
    for k in (1, 3, 2):
        remote(ph, phall.at[d], xs.at[0], xr.at[k - 1], at(0, 0, k, 0)).start()
    remote(ph, phall.at[d], ps.at[0], pr.at[0], at(0, 0, 0, 1)).start()
    pltpu.make_async_copy(ph, phall.at[d], own.at[4]).start()
    pltpu.make_async_copy(ph, phx.at[1], own.at[5]).start()
    start_z(KEY)
    start_z(VAL)
    start_z(OUT)

    def share():
        for k in (1, 3, 2):
            got = phall.at[((x + NX - k) % NX) * 2 + c]
            waited(got, xr.at[k - 1])
            remote(got, got, ps.at[0], pr.at[0], at(0, 0, 0, 1)).start()

    def mid(w):
        pltpu.make_async_copy(shards[w].at[:, columns], place(w), own.at[w]).wait()
        if w == OUT:
            waited(wo.at[x, c, pl.ds(0, NZ - 1), 0], zr.at[w])
            plane, dy, dx = wo.at[x, c, :, y], 1 - c, c
        else:
            waited(wb.at[w, pl.ds(0, NZ - 1), 0], zr.at[w])
            plane, dy, dx = wb.at[w, :, y], 1, 0
        for k in (2, 1, 3):
            remote(plane, plane, ms.at[w], mr.at[w], at(0, k * dy, k * dx, 0)).start()

    def portion(cc, k):
        if cc == 0:
            return wo.at[(x + NX - k) % NX, 0]
        return wo.at[:, 1, :, (y + NY - k) % NY]

    def each_core(body):
        for cc in range(2):
            pl.when(c == cc)(functools.partial(body, cc))

    def to_partner(ref):
        remote(ref, ref, cs.at[0], cr.at[0], at(0, 0, 0, 1)).start()

    def last():
        waited(wo.at[x, c, pl.ds(0, 12)], mr.at[OUT])

        def body(cc):
            mine = portion(cc, 0)
            for k in (1, 3, 2):
                remote(mine, mine, ls.at[0], lr.at[k - 1], at(0, k * cc, k * (1 - cc), 0)).start()
            to_partner(mine)

        each_core(body)

    def swap():
        def body(cc):
            for k in (1, 3, 2):
                waited(portion(cc, k), lr.at[k - 1])
                to_partner(portion(cc, k))

        each_core(body)

    def whole():
        waited(wo.at[:, 0], cr.at[0])

    def gather_phonemes():
        pltpu.make_async_copy(ph, phall.at[d], own.at[4]).wait()
        waited(phall.at[pl.ds(0, 4)], pr.at[0])
        for i in range(8):
            gall[i] = (phall[i].astype(jnp.float32) * gain[...]).astype(jnp.bfloat16)

    def deliver(w):
        waited(wb.at[w, pl.ds(0, 12)], mr.at[w])
        made = jnp.dot(gall[...].reshape(8 * PH, D), wb[w].reshape(D, 128), preferred_element_type=jnp.float32)
        sent[w] = made.astype(jnp.bfloat16).reshape(8, PH, 128)
        pltpu.make_async_copy(sent.at[w, d], pall.at[w, 1, d], own.at[6 + w]).start()

        def near(j, carry):
            remote(sent.at[w, (d + j) % 8], pall.at[w, 1, d], es.at[2 * w], er.at[2 * w], beside(0, j)).start()
            return carry

        def far(j, carry):
            mine = sent.at[w, (d + j) % 8]
            remote(mine, pall.at[w, 0, d], es.at[2 * w + 1], er.at[2 * w + 1], beside(1, j)).start()
            remote(mine, pall.at[w, 2, d], es.at[2 * w + 1], er.at[2 * w + 1], beside(-1, j)).start()
            return carry

        lax.fori_loop(0, 8, far, 0)
        lax.fori_loop(1, 8, near, 0)

    def upsample():
        waited(aux.at[0], arem.at[0])
        waited(aux.at[2], arem.at[1])
        cent = jnp.concatenate(
            [aux[0, 0:1, 0:PH] - FR, aux[1, 0:1, 0:PH], aux[2, 0:1, 0:PH] + FR], axis=1)
        sig = jnp.concatenate(
            [aux[0, 1:2, 0:PH], aux[1, 1:2, 0:PH], aux[2, 1:2, 0:PH]], axis=1)
        slot = lax.broadcasted_iota(jnp.int32, (1, 3 * PH), 1)
        usable = ((slot >= PH) | (s > 0)) & ((slot < 2 * PH) | (s < blocks - 1))
        reach = jnp.where(usable, RADIUS, -1.0)
        fall = -0.5 / (sig * sig)
        frame = lax.broadcasted_iota(jnp.int32, (KEYS, 3 * PH), 0).astype(jnp.float32) + (0.5 - WIN)
        gap = frame - cent
        band = jnp.where(jnp.abs(gap) <= reach, jnp.exp(gap * gap * fall), 0.0)
        total = jnp.sum(band, axis=1, keepdims=True)
        inv = jnp.where(total > 1e-16, 1.0 / total, 0.0)
        band_bf = band.astype(jnp.bfloat16)
        waited(phx.at[0], hr.at[0])
        waited(phx.at[2], hr.at[1])
        pltpu.make_async_copy(ph, phx.at[1], own.at[5]).wait()
        rows = phx[...].reshape(3 * PH, D)
        lifted = (jnp.dot(band_bf, rows, preferred_element_type=jnp.float32) * inv).astype(jnp.bfloat16)
        up[...] = lifted[WIN:WIN + FR]
        wide = lifted.astype(jnp.float32)
        norm = lax.rsqrt(jnp.mean(wide * wide, axis=1, keepdims=True) + 1e-6) * inv
        return band_bf, norm

    def project(w, band_rows, scale, dest):
        waited(pall.at[w, pl.ds(0, 2)], er.at[2 * w + 1])
        waited(pall.at[w, 0, pl.ds(0, 7)], er.at[2 * w])
        pltpu.make_async_copy(sent.at[w, d], pall.at[w, 1, d], own.at[6 + w]).wait()
        for g in range(4):
            part = jnp.concatenate(
                [pall[w, :, 2 * g].reshape(3 * PH, 128), pall[w, :, 2 * g + 1].reshape(3 * PH, 128)], axis=1)
            dest[:, g * GROUP:(g + 1) * GROUP] = (
                jnp.dot(band_rows, part, preferred_element_type=jnp.float32) * scale).astype(jnp.bfloat16)

    t_id = lax.broadcasted_iota(jnp.int32, (BLK, BLK), 0)
    u_id = lax.broadcasted_iota(jnp.int32, (BLK, BLK), 1)
    lane = lax.broadcasted_iota(jnp.int32, (BLK, GROUP), 1) // 64
    low = -1e30

    def weigh(g):
        lanes = slice(g * GROUP, (g + 1) * GROUP)
        for b in range(4):
            q4 = qs[b * BLK:(b + 1) * BLK, lanes]
            k4 = ks[b * BLK:b * BLK + SPAN, lanes]
            head = u_id >= t_id
            tail = u_id <= t_id
            if b == 0:
                head = head & (s > 0)
            if b == 3:
                tail = tail & (s < blocks - 1)
            head = jnp.where(head, 0.0, low)
            tail = jnp.where(tail, 0.0, low)
            stacked = jnp.concatenate([jnp.where(lane == h, q4, jnp.zeros_like(q4)) for h in range(4)], axis=0)
            scores = lax.dot_general(stacked, k4, (((1,), (1,)), ((), ())), preferred_element_type=jnp.float32)
            bias = jnp.concatenate([head, jnp.zeros((BLK, BLK), jnp.float32), tail], axis=1)
            scores = scores + jnp.concatenate([bias] * 4, axis=0)
            raised = jnp.exp2(scores - jnp.max(scores, axis=1, keepdims=True))
            scale = 1.0 / jnp.sum(raised, axis=1, keepdims=True)
            probs[g, b] = (raised * scale).astype(jnp.bfloat16)

    def mix(g):
        lanes = slice(g * GROUP, (g + 1) * GROUP)
        for b in range(4):
            v4 = vs[b * BLK:b * BLK + SPAN, lanes]
            mixed = jnp.dot(probs[g, b], v4, preferred_element_type=jnp.float32)
            got = jnp.zeros((BLK, GROUP), jnp.float32)
            for h in range(4):
                got = jnp.where(lane == h, mixed[h * BLK:(h + 1) * BLK], got)
            att[b * BLK:(b + 1) * BLK, lanes] = got.astype(jnp.bfloat16)

    def finish():
        for g in range(4):
            lanes = slice(g * GROUP, (g + 1) * GROUP)
            weight = jnp.concatenate(
                [wo[g, 0].reshape(D, 128), wo[g, 1].reshape(D, 128)], axis=1)
            out[:, lanes] = (
                jnp.dot(att[...], weight, preferred_element_type=jnp.float32)
                + up[:, lanes].astype(jnp.float32)).astype(jnp.bfloat16)

    share()
    mid(QRY)
    gather_phonemes()
    mid(KEY)
    deliver(QRY)
    mid(VAL)
    band_bf, norm = upsample()
    deliver(KEY)
    mid(OUT)
    deliver(VAL)
    last()
    project(QRY, band_bf[WIN:WIN + FR], norm[WIN:WIN + FR] * SCALE, qs)
    project(KEY, band_bf, norm, ks)
    weigh(0)
    weigh(1)
    swap()
    weigh(2)
    weigh(3)
    project(VAL, band_bf, norm, vs)
    for g in range(4):
        mix(g)
    whole()
    finish()

    for i in range(2):
        waited(auxs, asem.at[i])
        waited(ph, hs.at[i])
    waited(phall.at[pl.ds(0, 3)], xs.at[0])
    waited(phall.at[pl.ds(0, 4)], ps.at[0])
    for w in range(4):
        waited(wo.at[x, c, pl.ds(0, NZ - 1), 0], zs.at[w])
        waited(wo.at[x, c, pl.ds(0, 12)], ms.at[w])
    for w in range(3):
        waited(pall.at[w, 0, pl.ds(0, 7)], es.at[2 * w])
        waited(pall.at[w, pl.ds(0, 2)], es.at[2 * w + 1])
    waited(wo.at[pl.ds(0, 3), c], ls.at[0])
    waited(wo.at[:, c], cs.at[0])


def on_device(phonemes, spread, durations, norm_gain, w_query, w_key, w_value, w_out):
    vmem = pl.BlockSpec(memory_space=pltpu.VMEM)
    hbm = pl.BlockSpec(memory_space=pl.ANY)
    bf = jnp.bfloat16
    f32 = jnp.float32
    dma = pltpu.SemaphoreType.DMA
    return pl.pallas_call(
        kernel,
        out_shape=jax.ShapeDtypeStruct((FR, D), bf),
        in_specs=[hbm, vmem, vmem, vmem, hbm, hbm, hbm, hbm],
        out_specs=vmem,
        scratch_shapes=[
            pltpu.VMEM((3, NZ, NY, 16, 128), bf),
            pltpu.VMEM((NX, 2, NZ, NY, 16, 128), bf),
            pltpu.VMEM((3, PH, D), bf),
            pltpu.VMEM((8, PH, D), bf),
            pltpu.VMEM((8, PH, D), bf),
            pltpu.VMEM((3, 8, PH, 128), bf),
            pltpu.VMEM((3, 3, 8, PH, 128), bf),
            pltpu.VMEM((3, 8, 128), f32),
            pltpu.VMEM((8, 128), f32),
            pltpu.VMEM((FR, D), bf),
            pltpu.VMEM((FR, D), bf),
            pltpu.VMEM((KEYS, D), bf),
            pltpu.VMEM((KEYS, D), bf),
            pltpu.VMEM((4, 4, 4 * BLK, SPAN), bf),
            pltpu.VMEM((FR, D), bf),
            dma((4,)), dma((4,)), dma((4,)), dma((4,)), dma((1,)), dma((3,)),
            dma((1,)), dma((1,)), dma((9,)), dma((1,)), dma((3,)), dma((1,)), dma((1,)),
            dma((6,)), dma((6,)), dma((2,)), dma((2,)), dma((2,)), dma((2,)),
        ],
        compiler_params=pltpu.CompilerParams(
            collective_id=0, has_side_effects=True, vmem_limit_bytes=56 * 1024 * 1024),
        name="chapter_block",
    )(phonemes, spread.reshape(1, PH), durations, norm_gain.reshape(1, D),
      w_query, w_key, w_value, w_out)


def solution(mesh):
    placed = (
        P(("dp", "seq"), None),
        P(("dp", "seq")),
        P(("dp", "seq"), None),
        P(),
        P("seq", None),
        P("seq", None),
        P("seq", None),
        P("seq", None),
    )
    return jax.shard_map(
        on_device, mesh=mesh, in_specs=placed, out_specs=P(("dp", "seq"), None), check_vma=False
    )
```

```python
import math

import jax
import jax.numpy as jnp
from jax import lax
from jax.experimental import pallas as pl
from jax.experimental.pallas import tpu as pltpu
from jax.sharding import PartitionSpec as P

MESH = pl.DeviceIdType.MESH
NZ, NY, NX = 16, 4, 4
D = 1024
FR = 512
PH = 64
RADIUS = 32.0
WIN = 128
KEYS = FR + 2 * WIN
BLK = 128
SPAN = BLK + 2 * WIN
GROUP = 256
SCALE = math.log2(math.e) / 8.0
QRY, KEY, VAL, OUT = 0, 1, 2, 3


def kernel(ph, spread, dur, gain, w_qry, w_key, w_val, w_out, out,
           wb, wo, phx, phall, gall, sent, pall, aux, auxs, up, qs, ks, vs, probs, att,
           zs, zr, ms, mr, ls, lr, cs, cr, own, xs, xr, ps, pr, es, er, hs, hr, asem, arem):
    s = lax.axis_index("seq")
    d = lax.axis_index("dp")
    z, y, x, c = s // NY, s % NY, d // 2, d % 2
    shards = (w_qry, w_key, w_val, w_out)
    blocks = NZ * NY

    def at(dz, dy, dx, dc):
        zz, yy, xx, cc = (z + dz) % NZ, (y + dy) % NY, (x + dx) % NX, (c + dc) % 2
        return (zz * NY + yy, xx * 2 + cc)

    def beside(step, j):
        return ((s + blocks + step) % blocks, (d + j) % 8)

    columns = pl.ds(pl.multiple_of(d * 128, 128), 128)

    zh, zl = z // 4, z % 4
    low, high = pl.ds(0, 2), pl.ds(2, 2)
    mine = 2 + x % 2
    local = [pltpu.make_async_copy(shards[w].at[:, columns], wb.at[w, z, y], own.at[w]) for w in range(3)]
    for i, g in enumerate((0, 1, mine)):
        part = pl.ds(pl.multiple_of(g * GROUP + c * 128, 128), 128)
        local.append(pltpu.make_async_copy(w_out.at[:, part], wo.at[g, c, zh, zl, y], own.at[9 + i]))
    local.append(pltpu.make_async_copy(ph, phall.at[d], own.at[4]))
    local.append(pltpu.make_async_copy(ph, phx.at[1], own.at[5]))
    for copy in local:
        copy.start()

    barrier = pltpu.get_barrier_semaphore()

    def greet(dev):
        pl.semaphore_signal(barrier, inc=1, device_id=dev, device_id_type=MESH)

    for k in range(1, NZ):
        greet(at(k, 0, 0, 0))
    for k in range(1, NY):
        greet(at(0, k, 0, 0))
    for j in range(8):
        if j:
            greet(beside(0, j))
        greet(beside(1, j))
        greet(beside(-1, j))

    durf = dur[...].astype(jnp.float32)
    row = lax.broadcasted_iota(jnp.int32, (PH, PH), 0)
    col = lax.broadcasted_iota(jnp.int32, (PH, PH), 1)
    tri = jnp.where(row <= col, 1.0, 0.0).astype(jnp.bfloat16)
    ends = jnp.dot(jnp.broadcast_to(durf, (8, PH)).astype(jnp.bfloat16), tri,
                   preferred_element_type=jnp.float32)
    auxs[...] = jnp.zeros_like(auxs)
    auxs[0:1, 0:PH] = ends[0:1] - durf * 0.5
    auxs[1:2, 0:PH] = spread[...]
    aux[1] = auxs[...]

    pall[QRY, 0, :, 0:PH // 2] = jnp.zeros((8, PH // 2, 128), jnp.bfloat16)
    pall[QRY, 2, :, PH // 2:] = jnp.zeros((8, PH // 2, 128), jnp.bfloat16)
    for copy in local:
        copy.wait()
    pl.semaphore_wait(barrier, (NZ - 1) + (NY - 1) + 7 + 16)

    def remote(src, dst, ssem, rsem, dev):
        return pltpu.make_async_remote_copy(
            src_ref=src, dst_ref=dst, send_sem=ssem, recv_sem=rsem, device_id=dev, device_id_type=MESH)

    def waited(ref, sem):
        pltpu.make_async_copy(ref, ref, sem).wait()

    def start_z(w):
        piece = wo.at[mine, c, zh, zl, y] if w == OUT else wb.at[w, z, y]
        for k in (8, 7, 9, 6, 10, 5, 11, 4, 12, 3, 13, 2, 14, 1, 15):
            remote(piece, piece, zs.at[w], zr.at[w], at(k, 0, 0, 0)).start()

    for k in (2, 1, 3):
        remote(wo.at[low, c, zh, zl, y], wo.at[low, c, zh, zl, y], ls.at[0], lr.at[0], at(0, k, 0, 0)).start()
    start_z(QRY)
    for k in (1, 3, 2):
        remote(phall.at[d], phall.at[d], xs.at[0], xr.at[k - 1], at(0, 0, k, 0)).start()
    remote(auxs, aux.at[0], asem.at[0], arem.at[0], beside(1, 0)).start()
    remote(auxs, aux.at[2], asem.at[1], arem.at[1], beside(-1, 0)).start()
    remote(phall.at[d], phx.at[0], hs.at[0], hr.at[0], beside(1, 0)).start()
    remote(phall.at[d], phx.at[2], hs.at[1], hr.at[1], beside(-1, 0)).start()
    start_z(KEY)
    remote(phall.at[d], phall.at[d], ps.at[0], pr.at[0], at(0, 0, 0, 1)).start()
    start_z(VAL)
    start_z(OUT)

    def share():
        for k in (1, 3, 2):
            got = phall.at[((x + NX - k) % NX) * 2 + c]
            waited(got, xr.at[k - 1])
            remote(got, got, ps.at[0], pr.at[0], at(0, 0, 0, 1)).start()

    def mid(w):
        waited(wb.at[w, pl.ds(0, NZ - 1), 0], zr.at[w])
        for k in (2, 1, 3):
            remote(wb.at[w, :, y], wb.at[w, :, y], ms.at[w], mr.at[w], at(0, k, 0, 0)).start()

    def out_far():
        waited(wo.at[low, c, zh, zl, pl.ds(0, 3)], lr.at[0])
        ref = wo.at[low, c, zh, zl]
        for k in (8, 4, 12):
            remote(ref, ref, ls.at[1], lr.at[1], at(k, 0, 0, 0)).start()

    def out_near():
        waited(wo.at[low, c, pl.ds(0, 3), zl], lr.at[1])
        ref = wo.at[low, c, :, zl]
        for k in (2, 1, 15):
            remote(ref, ref, ls.at[2], lr.at[2], at(k, 0, 0, 0)).start()

    def out_pair():
        waited(wb.at[0, pl.ds(0, NZ - 1), 0], zr.at[OUT])
        ref = wo.at[mine, c, :, :, y]
        remote(ref, ref, ms.at[OUT], mr.at[OUT], at(0, 0, 1 + 2 * (x % 2), 0)).start()

    def out_plane():
        waited(wo.at[5 - mine, c, :, :, y], mr.at[OUT])
        ref = wo.at[high, c, :, :, y]
        for k in (2, 1, 3):
            remote(ref, ref, ls.at[3], lr.at[3], at(0, k, 0, 0)).start()

    def swap_low():
        waited(wo.at[low, c, :, pl.ds(0, 3)], lr.at[2])
        remote(wo.at[low, c], wo.at[low, c], cs.at[0], cr.at[0], at(0, 0, 0, 1)).start()

    def swap_high():
        waited(wo.at[high, c, :, :, pl.ds(0, 3)], lr.at[3])
        remote(wo.at[high, c], wo.at[high, c], cs.at[1], cr.at[1], at(0, 0, 0, 1)).start()

    def whole():
        waited(wo.at[low, 1 - c], cr.at[0])
        waited(wo.at[high, 1 - c], cr.at[1])

    def gather_phonemes():
        waited(phall.at[pl.ds(0, 4)], pr.at[0])
        for i in range(8):
            gall[i] = (phall[i].astype(jnp.float32) * gain[...]).astype(jnp.bfloat16)

    def reach_of(w):
        if w == QRY:
            return slice(PH // 2, PH), slice(0, PH // 2)
        return slice(0, PH), slice(0, PH)

    def far_bytes(w):
        return pall.at[w, 0] if w == QRY else pall.at[w, pl.ds(0, 2)]

    def deliver(w):
        waited(wb.at[w, pl.ds(0, 12)], mr.at[w])
        made = jnp.dot(gall[...].reshape(8 * PH, D), wb[w].reshape(D, 128), preferred_element_type=jnp.float32)
        sent[w] = made.astype(jnp.bfloat16).reshape(8, PH, 128)
        pltpu.make_async_copy(sent.at[w, d], pall.at[w, 1, d], own.at[6 + w]).start()

        def near(j, carry):
            remote(sent.at[w, (d + j) % 8], pall.at[w, 1, d], es.at[2 * w], er.at[2 * w], beside(0, j)).start()
            return carry

        late, early = reach_of(w)

        def far(j, carry):
            mine = sent.at[w, (d + j) % 8]
            remote(mine.at[late], pall.at[w, 0, d, late], es.at[2 * w + 1], er.at[2 * w + 1], beside(1, j)).start()
            remote(mine.at[early], pall.at[w, 2, d, early], es.at[2 * w + 1], er.at[2 * w + 1], beside(-1, j)).start()
            return carry

        lax.fori_loop(0, 8, far, 0)
        lax.fori_loop(1, 8, near, 0)

    def upsample():
        waited(aux.at[0], arem.at[0])
        waited(aux.at[2], arem.at[1])
        cent = jnp.concatenate(
            [aux[0, 0:1, 0:PH] - FR, aux[1, 0:1, 0:PH], aux[2, 0:1, 0:PH] + FR], axis=1)
        sig = jnp.concatenate(
            [aux[0, 1:2, 0:PH], aux[1, 1:2, 0:PH], aux[2, 1:2, 0:PH]], axis=1)
        slot = lax.broadcasted_iota(jnp.int32, (1, 3 * PH), 1)
        usable = ((slot >= PH) | (s > 0)) & ((slot < 2 * PH) | (s < blocks - 1))
        reach = jnp.where(usable, RADIUS, -1.0)
        fall = -0.5 / (sig * sig)
        frame = lax.broadcasted_iota(jnp.int32, (KEYS, 3 * PH), 0).astype(jnp.float32) + (0.5 - WIN)
        gap = frame - cent
        band = jnp.where(jnp.abs(gap) <= reach, jnp.exp(gap * gap * fall), 0.0)
        total = jnp.sum(band, axis=1, keepdims=True)
        inv = jnp.where(total > 1e-16, 1.0 / total, 0.0)
        band_bf = band.astype(jnp.bfloat16)
        waited(phx.at[0], hr.at[0])
        waited(phx.at[2], hr.at[1])
        rows = phx[...].reshape(3 * PH, D)
        lifted = (jnp.dot(band_bf, rows, preferred_element_type=jnp.float32) * inv).astype(jnp.bfloat16)
        up[...] = lifted[WIN:WIN + FR]
        wide = lifted.astype(jnp.float32)
        norm = lax.rsqrt(jnp.mean(wide * wide, axis=1, keepdims=True) + 1e-6) * inv
        return band_bf, norm

    def project(w, band_rows, scale, dest):
        waited(far_bytes(w), er.at[2 * w + 1])
        waited(pall.at[w, 0, pl.ds(0, 7)], er.at[2 * w])
        pltpu.make_async_copy(sent.at[w, d], pall.at[w, 1, d], own.at[6 + w]).wait()
        for g in range(4):
            part = jnp.concatenate(
                [pall[w, :, 2 * g].reshape(3 * PH, 128), pall[w, :, 2 * g + 1].reshape(3 * PH, 128)], axis=1)
            dest[:, g * GROUP:(g + 1) * GROUP] = (
                jnp.dot(band_rows, part, preferred_element_type=jnp.float32) * scale).astype(jnp.bfloat16)

    t_id = lax.broadcasted_iota(jnp.int32, (BLK, BLK), 0)
    u_id = lax.broadcasted_iota(jnp.int32, (BLK, BLK), 1)
    lane = lax.broadcasted_iota(jnp.int32, (BLK, GROUP), 1) // 64
    never = -1e30

    def weigh(g):
        lanes = slice(g * GROUP, (g + 1) * GROUP)
        for b in range(4):
            q4 = qs[b * BLK:(b + 1) * BLK, lanes]
            k4 = ks[b * BLK:b * BLK + SPAN, lanes]
            head = u_id >= t_id
            tail = u_id <= t_id
            if b == 0:
                head = head & (s > 0)
            if b == 3:
                tail = tail & (s < blocks - 1)
            head = jnp.where(head, 0.0, never)
            tail = jnp.where(tail, 0.0, never)
            stacked = jnp.concatenate([jnp.where(lane == h, q4, jnp.zeros_like(q4)) for h in range(4)], axis=0)
            scores = lax.dot_general(stacked, k4, (((1,), (1,)), ((), ())), preferred_element_type=jnp.float32)
            bias = jnp.concatenate([head, jnp.zeros((BLK, BLK), jnp.float32), tail], axis=1)
            scores = scores + jnp.concatenate([bias] * 4, axis=0)
            raised = jnp.exp2(scores - jnp.max(scores, axis=1, keepdims=True))
            scale = 1.0 / jnp.sum(raised, axis=1, keepdims=True)
            probs[g, b] = (raised * scale).astype(jnp.bfloat16)

    def mix(g):
        lanes = slice(g * GROUP, (g + 1) * GROUP)
        for b in range(4):
            v4 = vs[b * BLK:b * BLK + SPAN, lanes]
            mixed = jnp.dot(probs[g, b], v4, preferred_element_type=jnp.float32)
            got = jnp.zeros((BLK, GROUP), jnp.float32)
            for h in range(4):
                got = jnp.where(lane == h, mixed[h * BLK:(h + 1) * BLK], got)
            att[b * BLK:(b + 1) * BLK, lanes] = got.astype(jnp.bfloat16)

    def finish():
        for g in range(4):
            lanes = slice(g * GROUP, (g + 1) * GROUP)
            weight = jnp.concatenate(
                [wo[g, 0].reshape(D, 128), wo[g, 1].reshape(D, 128)], axis=1)
            out[:, lanes] = (
                jnp.dot(att[...], weight, preferred_element_type=jnp.float32)
                + up[:, lanes].astype(jnp.float32)).astype(jnp.bfloat16)

    out_far()
    mid(QRY)
    mid(KEY)
    share()
    mid(VAL)
    gather_phonemes()
    deliver(QRY)
    out_pair()
    deliver(KEY)
    deliver(VAL)
    out_plane()
    out_near()
    band_bf, norm = upsample()
    project(QRY, band_bf[WIN:WIN + FR], norm[WIN:WIN + FR] * SCALE, qs)
    project(KEY, band_bf, norm, ks)
    weigh(0)
    weigh(1)
    swap_high()
    swap_low()
    weigh(2)
    weigh(3)
    project(VAL, band_bf, norm, vs)
    for g in range(4):
        mix(g)
    whole()
    finish()

    for i in range(2):
        waited(auxs, asem.at[i])
        waited(phx.at[1], hs.at[i])
    waited(phall.at[pl.ds(0, 3)], xs.at[0])
    waited(phall.at[pl.ds(0, 4)], ps.at[0])
    for w in range(4):
        waited(wb.at[0, pl.ds(0, NZ - 1), 0], zs.at[w])
    for w in range(3):
        waited(wb.at[w, pl.ds(0, 12)], ms.at[w])
        waited(pall.at[w, 0, pl.ds(0, 7)], es.at[2 * w])
        waited(far_bytes(w), es.at[2 * w + 1])
    waited(wo.at[mine, c, :, :, y], ms.at[OUT])
    waited(wo.at[low, c, zh, zl, pl.ds(0, 3)], ls.at[0])
    waited(wo.at[low, c, pl.ds(0, 3), zl], ls.at[1])
    waited(wo.at[low, c, :, pl.ds(0, 3)], ls.at[2])
    waited(wo.at[high, c, :, :, pl.ds(0, 3)], ls.at[3])
    waited(wo.at[low, c], cs.at[0])
    waited(wo.at[high, c], cs.at[1])


def on_device(phonemes, spread, durations, norm_gain, w_query, w_key, w_value, w_out):
    vmem = pl.BlockSpec(memory_space=pltpu.VMEM)
    hbm = pl.BlockSpec(memory_space=pl.ANY)
    bf = jnp.bfloat16
    f32 = jnp.float32
    dma = pltpu.SemaphoreType.DMA
    return pl.pallas_call(
        kernel,
        out_shape=jax.ShapeDtypeStruct((FR, D), bf),
        in_specs=[hbm, vmem, vmem, vmem, hbm, hbm, hbm, hbm],
        out_specs=vmem,
        scratch_shapes=[
            pltpu.VMEM((3, NZ, NY, 16, 128), bf),
            pltpu.VMEM((4, 2, 4, 4, NY, 16, 128), bf),
            pltpu.VMEM((3, PH, D), bf),
            pltpu.VMEM((8, PH, D), bf),
            pltpu.VMEM((8, PH, D), bf),
            pltpu.VMEM((3, 8, PH, 128), bf),
            pltpu.VMEM((3, 3, 8, PH, 128), bf),
            pltpu.VMEM((3, 8, 128), f32),
            pltpu.VMEM((8, 128), f32),
            pltpu.VMEM((FR, D), bf),
            pltpu.VMEM((FR, D), bf),
            pltpu.VMEM((KEYS, D), bf),
            pltpu.VMEM((KEYS, D), bf),
            pltpu.VMEM((4, 4, 4 * BLK, SPAN), bf),
            pltpu.VMEM((FR, D), bf),
            dma((4,)), dma((4,)), dma((4,)), dma((4,)), dma((4,)), dma((4,)),
            dma((2,)), dma((2,)), dma((12,)), dma((1,)), dma((3,)), dma((1,)), dma((1,)),
            dma((6,)), dma((6,)), dma((2,)), dma((2,)), dma((2,)), dma((2,)),
        ],
        compiler_params=pltpu.CompilerParams(
            collective_id=0, has_side_effects=True, vmem_limit_bytes=56 * 1024 * 1024),
        name="chapter_block",
    )(phonemes, spread.reshape(1, PH), durations, norm_gain.reshape(1, D),
      w_query, w_key, w_value, w_out)


def solution(mesh):
    placed = (
        P(("dp", "seq"), None),
        P(("dp", "seq")),
        P(("dp", "seq"), None),
        P(),
        P("seq", None),
        P("seq", None),
        P("seq", None),
        P("seq", None),
    )
    return jax.shard_map(
        on_device, mesh=mesh, in_specs=placed, out_specs=P(("dp", "seq"), None), check_vma=False
    )
```

```python
import math

import jax
import jax.numpy as jnp
from jax import lax
from jax.experimental import pallas as pl
from jax.experimental.pallas import tpu as pltpu
from jax.sharding import PartitionSpec as P

MESH = pl.DeviceIdType.MESH
NZ, NY, NX = 16, 4, 4
D = 1024
FR = 512
PH = 64
RADIUS = 32.0
WIN = 128
KEYS = FR + 2 * WIN
BLK = 128
SPAN = BLK + 2 * WIN
GROUP = 256
SCALE = math.log2(math.e) / 8.0
QRY, KEY, VAL, OUT = 0, 1, 2, 3


def kernel(ph, spread, dur, gain, w_qry, w_key, w_val, w_out, out,
           wb, wo, phx, phall, gall, sent, pall, aux, auxs, up, qs, ks, vs, probs, att,
           zs, zr, ms, mr, ls, lr, cs, cr, own, xs, xr, ps, pr, es, er, hs, hr, asem, arem):
    s = lax.axis_index("seq")
    d = lax.axis_index("dp")
    z, y, x, c = s // NY, s % NY, d // 2, d % 2
    shards = (w_qry, w_key, w_val, w_out)
    blocks = NZ * NY

    def at(dz, dy, dx, dc):
        zz, yy, xx, cc = (z + dz) % NZ, (y + dy) % NY, (x + dx) % NX, (c + dc) % 2
        return (zz * NY + yy, xx * 2 + cc)

    def beside(step, j):
        return ((s + blocks + step) % blocks, (d + j) % 8)

    columns = pl.ds(pl.multiple_of(d * 128, 128), 128)

    zh, zl = z // 4, z % 4
    low, high = pl.ds(0, 2), pl.ds(2, 2)
    mine = 2 + x % 2
    local = [pltpu.make_async_copy(shards[w].at[:, columns], wb.at[w, z, y], own.at[w]) for w in range(3)]
    for i, g in enumerate((0, 1, mine)):
        part = pl.ds(pl.multiple_of(g * GROUP + c * 128, 128), 128)
        local.append(pltpu.make_async_copy(w_out.at[:, part], wo.at[g, c, zh, zl, y], own.at[9 + i]))
    local.append(pltpu.make_async_copy(ph, phall.at[d], own.at[4]))
    local.append(pltpu.make_async_copy(ph, phx.at[1], own.at[5]))
    for copy in local:
        copy.start()

    barrier = pltpu.get_barrier_semaphore()

    def greet(dev):
        pl.semaphore_signal(barrier, inc=1, device_id=dev, device_id_type=MESH)

    for k in range(1, NZ):
        greet(at(k, 0, 0, 0))
    for k in range(1, NY):
        greet(at(0, k, 0, 0))
    for j in range(8):
        if j:
            greet(beside(0, j))
        greet(beside(1, j))
        greet(beside(-1, j))

    durf = dur[...].astype(jnp.float32)
    row = lax.broadcasted_iota(jnp.int32, (PH, PH), 0)
    col = lax.broadcasted_iota(jnp.int32, (PH, PH), 1)
    tri = jnp.where(row <= col, 1.0, 0.0).astype(jnp.bfloat16)
    ends = jnp.dot(jnp.broadcast_to(durf, (8, PH)).astype(jnp.bfloat16), tri,
                   preferred_element_type=jnp.float32)
    auxs[...] = jnp.zeros_like(auxs)
    auxs[0:1, 0:PH] = ends[0:1] - durf * 0.5
    auxs[1:2, 0:PH] = spread[...]
    aux[1] = auxs[...]

    pall[QRY, 0, :, 0:PH // 2] = jnp.zeros((8, PH // 2, 128), jnp.bfloat16)
    pall[QRY, 2, :, PH // 2:] = jnp.zeros((8, PH // 2, 128), jnp.bfloat16)
    for copy in local:
        copy.wait()
    pl.semaphore_wait(barrier, (NZ - 1) + (NY - 1) + 7 + 16)

    def remote(src, dst, ssem, rsem, dev):
        return pltpu.make_async_remote_copy(
            src_ref=src, dst_ref=dst, send_sem=ssem, recv_sem=rsem, device_id=dev, device_id_type=MESH)

    def waited(ref, sem):
        pltpu.make_async_copy(ref, ref, sem).wait()

    def start_z(w):
        piece = wo.at[mine, c, zh, zl, y] if w == OUT else wb.at[w, z, y]
        for k in (8, 7, 9, 6, 10, 5, 11, 4, 12, 3, 13, 2, 14, 1, 15):
            remote(piece, piece, zs.at[w], zr.at[w], at(k, 0, 0, 0)).start()

    for k in (2, 1, 3):
        remote(wo.at[low, c, zh, zl, y], wo.at[low, c, zh, zl, y], ls.at[0], lr.at[0], at(0, k, 0, 0)).start()
    start_z(QRY)
    for k in (1, 3, 2):
        remote(phall.at[d], phall.at[d], xs.at[0], xr.at[k - 1], at(0, 0, k, 0)).start()
    remote(auxs, aux.at[0], asem.at[0], arem.at[0], beside(1, 0)).start()
    remote(auxs, aux.at[2], asem.at[1], arem.at[1], beside(-1, 0)).start()
    remote(phall.at[d], phx.at[0], hs.at[0], hr.at[0], beside(1, 0)).start()
    remote(phall.at[d], phx.at[2], hs.at[1], hr.at[1], beside(-1, 0)).start()
    start_z(KEY)
    remote(phall.at[d], phall.at[d], ps.at[0], pr.at[0], at(0, 0, 0, 1)).start()
    start_z(VAL)
    start_z(OUT)

    def share():
        for k in (1, 3, 2):
            got = phall.at[((x + NX - k) % NX) * 2 + c]
            waited(got, xr.at[k - 1])
            remote(got, got, ps.at[0], pr.at[0], at(0, 0, 0, 1)).start()

    def mid(w):
        waited(wb.at[w, pl.ds(0, NZ - 1), 0], zr.at[w])
        for k in (2, 1, 3):
            remote(wb.at[w, :, y], wb.at[w, :, y], ms.at[w], mr.at[w], at(0, k, 0, 0)).start()

    def out_far():
        waited(wo.at[low, c, zh, zl, pl.ds(0, 3)], lr.at[0])
        ref = wo.at[low, c, zh, zl]
        for k in (8, 4, 12):
            remote(ref, ref, ls.at[1], lr.at[1], at(k, 0, 0, 0)).start()

    def out_near():
        waited(wo.at[low, c, pl.ds(0, 3), zl], lr.at[1])
        ref = wo.at[low, c, :, zl]
        for k in (2, 1, 15):
            remote(ref, ref, ls.at[2], lr.at[2], at(k, 0, 0, 0)).start()

    def out_pair():
        waited(wb.at[0, pl.ds(0, NZ - 1), 0], zr.at[OUT])
        ref = wo.at[mine, c, :, :, y]
        remote(ref, ref, ms.at[OUT], mr.at[OUT], at(0, 0, 1 + 2 * (x % 2), 0)).start()

    def out_plane():
        waited(wo.at[5 - mine, c, :, :, y], mr.at[OUT])
        ref = wo.at[high, c, :, :, y]
        for k in (2, 1, 3):
            remote(ref, ref, ls.at[3], lr.at[3], at(0, k, 0, 0)).start()

    def swap_low():
        waited(wo.at[low, c, :, pl.ds(0, 3)], lr.at[2])
        remote(wo.at[low, c], wo.at[low, c], cs.at[0], cr.at[0], at(0, 0, 0, 1)).start()

    def swap_high():
        waited(wo.at[high, c, :, :, pl.ds(0, 3)], lr.at[3])
        remote(wo.at[high, c], wo.at[high, c], cs.at[1], cr.at[1], at(0, 0, 0, 1)).start()

    def whole(part, i):
        waited(wo.at[part, 1 - c], cr.at[i])

    def gather_phonemes():
        waited(phall.at[pl.ds(0, 4)], pr.at[0])
        for i in range(8):
            gall[i] = (phall[i].astype(jnp.float32) * gain[...]).astype(jnp.bfloat16)

    def reach_of(w):
        if w == QRY:
            return slice(PH // 2, PH), slice(0, PH // 2)
        return slice(0, PH), slice(0, PH)

    def far_bytes(w):
        return pall.at[w, 0] if w == QRY else pall.at[w, pl.ds(0, 2)]

    def deliver(w):
        waited(wb.at[w, pl.ds(0, 12)], mr.at[w])
        made = jnp.dot(gall[...].reshape(8 * PH, D), wb[w].reshape(D, 128), preferred_element_type=jnp.float32)
        sent[w] = made.astype(jnp.bfloat16).reshape(8, PH, 128)
        pltpu.make_async_copy(sent.at[w, d], pall.at[w, 1, d], own.at[6 + w]).start()

        def near(j, carry):
            remote(sent.at[w, (d + j) % 8], pall.at[w, 1, d], es.at[2 * w], er.at[2 * w], beside(0, j)).start()
            return carry

        late, early = reach_of(w)

        def far(j, carry):
            mine = sent.at[w, (d + j) % 8]
            remote(mine.at[late], pall.at[w, 0, d, late], es.at[2 * w + 1], er.at[2 * w + 1], beside(1, j)).start()
            remote(mine.at[early], pall.at[w, 2, d, early], es.at[2 * w + 1], er.at[2 * w + 1], beside(-1, j)).start()
            return carry

        lax.fori_loop(0, 8, far, 0)
        lax.fori_loop(1, 8, near, 0)

    def upsample():
        waited(aux.at[0], arem.at[0])
        waited(aux.at[2], arem.at[1])
        cent = jnp.concatenate(
            [aux[0, 0:1, 0:PH] - FR, aux[1, 0:1, 0:PH], aux[2, 0:1, 0:PH] + FR], axis=1)
        sig = jnp.concatenate(
            [aux[0, 1:2, 0:PH], aux[1, 1:2, 0:PH], aux[2, 1:2, 0:PH]], axis=1)
        slot = lax.broadcasted_iota(jnp.int32, (1, 3 * PH), 1)
        usable = ((slot >= PH) | (s > 0)) & ((slot < 2 * PH) | (s < blocks - 1))
        reach = jnp.where(usable, RADIUS, -1.0)
        fall = -0.5 / (sig * sig)
        frame = lax.broadcasted_iota(jnp.int32, (KEYS, 3 * PH), 0).astype(jnp.float32) + (0.5 - WIN)
        gap = frame - cent
        band = jnp.where(jnp.abs(gap) <= reach, jnp.exp(gap * gap * fall), 0.0)
        total = jnp.sum(band, axis=1, keepdims=True)
        inv = jnp.where(total > 1e-16, 1.0 / total, 0.0)
        band_bf = band.astype(jnp.bfloat16)
        waited(phx.at[0], hr.at[0])
        waited(phx.at[2], hr.at[1])
        rows = phx[...].reshape(3 * PH, D)
        lifted = (jnp.dot(band_bf, rows, preferred_element_type=jnp.float32) * inv).astype(jnp.bfloat16)
        up[...] = lifted[WIN:WIN + FR]
        wide = lifted.astype(jnp.float32)
        norm = lax.rsqrt(jnp.mean(wide * wide, axis=1, keepdims=True) + 1e-6) * inv
        return band_bf, norm

    def project(w, band_rows, scale, dest):
        waited(far_bytes(w), er.at[2 * w + 1])
        waited(pall.at[w, 0, pl.ds(0, 7)], er.at[2 * w])
        pltpu.make_async_copy(sent.at[w, d], pall.at[w, 1, d], own.at[6 + w]).wait()
        for g in range(4):
            part = jnp.concatenate(
                [pall[w, :, 2 * g].reshape(3 * PH, 128), pall[w, :, 2 * g + 1].reshape(3 * PH, 128)], axis=1)
            dest[:, g * GROUP:(g + 1) * GROUP] = (
                jnp.dot(band_rows, part, preferred_element_type=jnp.float32) * scale).astype(jnp.bfloat16)

    t_id = lax.broadcasted_iota(jnp.int32, (BLK, BLK), 0)
    u_id = lax.broadcasted_iota(jnp.int32, (BLK, BLK), 1)
    lane = lax.broadcasted_iota(jnp.int32, (BLK, GROUP), 1) // 64
    never = -1e30

    def weigh(g):
        lanes = slice(g * GROUP, (g + 1) * GROUP)
        for b in range(4):
            q4 = qs[b * BLK:(b + 1) * BLK, lanes]
            k4 = ks[b * BLK:b * BLK + SPAN, lanes]
            head = u_id >= t_id
            tail = u_id <= t_id
            if b == 0:
                head = head & (s > 0)
            if b == 3:
                tail = tail & (s < blocks - 1)
            head = jnp.where(head, 0.0, never)
            tail = jnp.where(tail, 0.0, never)
            stacked = jnp.concatenate([jnp.where(lane == h, q4, jnp.zeros_like(q4)) for h in range(4)], axis=0)
            scores = lax.dot_general(stacked, k4, (((1,), (1,)), ((), ())), preferred_element_type=jnp.float32)
            bias = jnp.concatenate([head, jnp.zeros((BLK, BLK), jnp.float32), tail], axis=1)
            scores = scores + jnp.concatenate([bias] * 4, axis=0)
            raised = jnp.exp2(scores - jnp.max(scores, axis=1, keepdims=True))
            scale = 1.0 / jnp.sum(raised, axis=1, keepdims=True)
            probs[g, b] = (raised * scale).astype(jnp.bfloat16)

    def mix(g):
        lanes = slice(g * GROUP, (g + 1) * GROUP)
        for b in range(4):
            v4 = vs[b * BLK:b * BLK + SPAN, lanes]
            mixed = jnp.dot(probs[g, b], v4, preferred_element_type=jnp.float32)
            got = jnp.zeros((BLK, GROUP), jnp.float32)
            for h in range(4):
                got = jnp.where(lane == h, mixed[h * BLK:(h + 1) * BLK], got)
            att[b * BLK:(b + 1) * BLK, lanes] = got.astype(jnp.bfloat16)

    def finish(groups):
        for g in groups:
            lanes = slice(g * GROUP, (g + 1) * GROUP)
            weight = jnp.concatenate(
                [wo[g, 0].reshape(D, 128), wo[g, 1].reshape(D, 128)], axis=1)
            out[:, lanes] = (
                jnp.dot(att[...], weight, preferred_element_type=jnp.float32)
                + up[:, lanes].astype(jnp.float32)).astype(jnp.bfloat16)

    out_far()
    mid(QRY)
    mid(KEY)
    share()
    mid(VAL)
    gather_phonemes()
    deliver(QRY)
    out_pair()
    deliver(KEY)
    deliver(VAL)
    out_plane()
    out_near()
    band_bf, norm = upsample()
    project(QRY, band_bf[WIN:WIN + FR], norm[WIN:WIN + FR] * SCALE, qs)
    project(KEY, band_bf, norm, ks)
    weigh(0)
    weigh(1)
    weigh(2)
    weigh(3)
    swap_high()
    project(VAL, band_bf, norm, vs)
    mix(0)
    mix(1)
    swap_low()
    mix(2)
    mix(3)
    whole(high, 1)
    finish((2, 3))
    whole(low, 0)
    finish((0, 1))

    for i in range(2):
        waited(auxs, asem.at[i])
        waited(phx.at[1], hs.at[i])
    waited(phall.at[pl.ds(0, 3)], xs.at[0])
    waited(phall.at[pl.ds(0, 4)], ps.at[0])
    for w in range(4):
        waited(wb.at[0, pl.ds(0, NZ - 1), 0], zs.at[w])
    for w in range(3):
        waited(wb.at[w, pl.ds(0, 12)], ms.at[w])
        waited(pall.at[w, 0, pl.ds(0, 7)], es.at[2 * w])
        waited(far_bytes(w), es.at[2 * w + 1])
    waited(wo.at[mine, c, :, :, y], ms.at[OUT])
    waited(wo.at[low, c, zh, zl, pl.ds(0, 3)], ls.at[0])
    waited(wo.at[low, c, pl.ds(0, 3), zl], ls.at[1])
    waited(wo.at[low, c, :, pl.ds(0, 3)], ls.at[2])
    waited(wo.at[high, c, :, :, pl.ds(0, 3)], ls.at[3])
    waited(wo.at[low, c], cs.at[0])
    waited(wo.at[high, c], cs.at[1])


def on_device(phonemes, spread, durations, norm_gain, w_query, w_key, w_value, w_out):
    vmem = pl.BlockSpec(memory_space=pltpu.VMEM)
    hbm = pl.BlockSpec(memory_space=pl.ANY)
    bf = jnp.bfloat16
    f32 = jnp.float32
    dma = pltpu.SemaphoreType.DMA
    return pl.pallas_call(
        kernel,
        out_shape=jax.ShapeDtypeStruct((FR, D), bf),
        in_specs=[hbm, vmem, vmem, vmem, hbm, hbm, hbm, hbm],
        out_specs=vmem,
        scratch_shapes=[
            pltpu.VMEM((3, NZ, NY, 16, 128), bf),
            pltpu.VMEM((4, 2, 4, 4, NY, 16, 128), bf),
            pltpu.VMEM((3, PH, D), bf),
            pltpu.VMEM((8, PH, D), bf),
            pltpu.VMEM((8, PH, D), bf),
            pltpu.VMEM((3, 8, PH, 128), bf),
            pltpu.VMEM((3, 3, 8, PH, 128), bf),
            pltpu.VMEM((3, 8, 128), f32),
            pltpu.VMEM((8, 128), f32),
            pltpu.VMEM((FR, D), bf),
            pltpu.VMEM((FR, D), bf),
            pltpu.VMEM((KEYS, D), bf),
            pltpu.VMEM((KEYS, D), bf),
            pltpu.VMEM((4, 4, 4 * BLK, SPAN), bf),
            pltpu.VMEM((FR, D), bf),
            dma((4,)), dma((4,)), dma((4,)), dma((4,)), dma((4,)), dma((4,)),
            dma((2,)), dma((2,)), dma((12,)), dma((1,)), dma((3,)), dma((1,)), dma((1,)),
            dma((6,)), dma((6,)), dma((2,)), dma((2,)), dma((2,)), dma((2,)),
        ],
        compiler_params=pltpu.CompilerParams(
            collective_id=0, has_side_effects=True, vmem_limit_bytes=56 * 1024 * 1024),
        name="chapter_block",
    )(phonemes, spread.reshape(1, PH), durations, norm_gain.reshape(1, D),
      w_query, w_key, w_value, w_out)


def solution(mesh):
    placed = (
        P(("dp", "seq"), None),
        P(("dp", "seq")),
        P(("dp", "seq"), None),
        P(),
        P("seq", None),
        P("seq", None),
        P("seq", None),
        P("seq", None),
    )
    return jax.shard_map(
        on_device, mesh=mesh, in_specs=placed, out_specs=P(("dp", "seq"), None), check_vma=False
    )
```
